32 devices in a mesh: rep: 4 (over y, core), fsdp: 8 (over z, x).
Axes of the slice: x: 2, y: 2, z: 4, core: 2. Of those that a mesh axis runs over, the one named last changes fastest.
Arguments:
- tokens: bfloat16 [16384, 1024], P(('rep', 'fsdp')), may hold values from -6 to 6
- segment: int32 [16384], P(('rep', 'fsdp')), may hold values from -1 to 9, as said below
- cotangent: bfloat16 [16384, 1024], P(('rep', 'fsdp')), may hold values from -6 to 6
- attn_norm_gain: bfloat16 [1024], P('fsdp'), may hold values from 0.5 to 1.5
- attn_norm_bias: bfloat16 [1024], P('fsdp'), may hold values from -1.75 to 1.75
- qkv_weight: bfloat16 [1024, 3072], P('fsdp'), may hold values from -0.1875 to 0.1875
- query_bias: bfloat16 [1024], P('fsdp'), may hold values from -3 to 3
- value_bias: bfloat16 [1024], P('fsdp'), may hold values from -3 to 3
- proj_weight: bfloat16 [1024, 1024], P('fsdp'), may hold values from -4 to 4
- proj_bias: bfloat16 [1024], P('fsdp'), may hold values from -1.75 to 1.75
- attn_scale: bfloat16 [1024], P('fsdp'), may hold values from 0.29882812 to 1.5
- mlp_norm_gain: bfloat16 [1024], P('fsdp'), may hold values from 0.5 to 1.5
- mlp_norm_bias: bfloat16 [1024], P('fsdp'), may hold values from -1.75 to 1.75
- hidden_weight: bfloat16 [1024, 4096], P('fsdp'), may hold values from -0.1875 to 0.1875
- hidden_bias: bfloat16 [4096], P('fsdp'), may hold values from -1.75 to 1.75
- output_weight: bfloat16 [4096, 1024], P('fsdp'), may hold values from -0.09375 to 0.09375
- output_bias: bfloat16 [1024], P('fsdp'), may hold values from -1.75 to 1.75
- mlp_scale: bfloat16 [1024], P('fsdp'), may hold values from 0.29882812 to 1.5
Outputs:
- block_output: bfloat16 [16384, 1024], P(('rep', 'fsdp'))
- input_grad: float32 [16384, 1024], P(('rep', 'fsdp'))
- attn_norm_gain_grad: float32 [1024], P('fsdp')
- attn_norm_bias_grad: float32 [1024], P('fsdp')
- qkv_weight_grad: float32 [1024, 3072], P('fsdp')
- query_bias_grad: float32 [1024], P('fsdp')
- value_bias_grad: float32 [1024], P('fsdp')
- proj_weight_grad: float32 [1024, 1024], P('fsdp')
- proj_bias_grad: float32 [1024], P('fsdp')
- attn_scale_grad: float32 [1024], P('fsdp')
- mlp_norm_gain_grad: float32 [1024], P('fsdp')
- mlp_norm_bias_grad: float32 [1024], P('fsdp')
- hidden_weight_grad: float32 [1024, 4096], P('fsdp')
- hidden_bias_grad: float32 [4096], P('fsdp')
- output_weight_grad: float32 [4096, 1024], P('fsdp')
- output_bias_grad: float32 [1024], P('fsdp')
- mlp_scale_grad: float32 [1024], P('fsdp')
The draws below stay inside these ranges and needn't reach their ends.
Inputs may be any that keep to these rules, and one draw needn't show every extreme that they name: `segment`: image k (0 to 9) is a run of exactly 1370 consecutive tokens that starts after image k - 1 ends; -1 marks padding tokens between the images; image 0 starts at token 0; some image starts at the last token of a device's rows, so it extends 3 devices further; the last image starts at token 14847.
All inputs are finite; a program needn't handle non-finite values.
Results may differ from the reference program's by a relative error of at most 0.02.
Values may be sent and summed in bfloat16 or wider, within the bound.
A program may use at most 256 MiB of HBM per device.

```python
import math
import jax
import jax.numpy as jnp
from jax import lax

D = 1024
H = 16
HD = 64
FF = 4096
TOK_DEV = 512
IMG_LEN = 1370
GAP = 32
REACH = 3
TOKENS = 16384
NIMG = 10


def draw_segment(key, part):
    key = jax.random.fold_in(key, 7)
    gap_key, pick_key = jax.random.split(key)
    number = jnp.arange(NIMG, dtype=jnp.int32)
    gap_sizes = jax.random.randint(gap_key, (NIMG,), 0, GAP + 1, dtype=jnp.int32)
    gap_sizes = jnp.where(number > 0, gap_sizes, 0)
    chosen = jax.random.randint(pick_key, (), 1, NIMG - 1, dtype=jnp.int32)
    starts = number * IMG_LEN + jnp.cumsum(gap_sizes).astype(jnp.int32)
    anchor = jnp.sum(jnp.where(number == chosen, starts, 0))
    offset = (TOK_DEV - 1 - anchor) % TOK_DEV
    starts = starts + jnp.where(number >= chosen, offset, 0)
    starts = jnp.where(number == NIMG - 1, TOKENS - REACH * TOK_DEV - 1, starts)
    position = jnp.arange(TOKENS, dtype=jnp.int32)
    inside = (position[:, None] >= starts[None, :]) & (position[:, None] < starts[None, :] + IMG_LEN)
    labels = jnp.sum(jnp.where(inside, number[None, :] + 1, 0), axis=1)
    return (labels - 1).astype(jnp.int32)


def strengthened(array, rng, source, target, blocks, factor):
    owner, partner = [(jnp.arange(array.shape[dim]) // (array.shape[dim] // blocks)).reshape([-1 if axis == dim else 1 for axis in range(array.ndim)]) for dim in (source, target)]
    chosen = jax.random.permutation(rng, blocks)[partner]
    strong = (owner == chosen) | (owner == (partner + blocks // 2) % blocks)
    return jnp.where(strong, factor * array, array)


def block_scale(stream_key, extent, cuts, smallest, largest):
    loudness = 1.0
    for dim, shards_of in cuts:
        draws = jax.random.uniform(jax.random.fold_in(jax.random.fold_in(stream_key, 6), dim), (shards_of,), jnp.float32, smallest / len(cuts), largest / len(cuts))
        loudness = loudness * jnp.repeat(jnp.exp(draws), extent[dim] // shards_of).reshape((-1,) + (1,) * (len(extent) - 1 - dim))
    return loudness


def noise(own_key, shape, deviation, limit, cuts=(), held_as=jnp.bfloat16):
    values = jax.random.normal(own_key, shape, jnp.float32) * deviation
    if len(cuts) > 0:
        values = block_scale(own_key, shape, cuts, -0.22, 0.18) * values
    return jnp.clip(values, min=-limit, max=limit).astype(held_as)


def gaussian_with(rng, dims, width, reach, pieces, heavy, kind=jnp.bfloat16):
    drawn = width * jax.random.normal(rng, dims, jnp.float32)
    if pieces:
        drawn = drawn * block_scale(rng, dims, pieces, -0.22, 0.18)
    return jnp.clip(strengthened(drawn, jax.random.fold_in(rng, 3), *heavy), -reach, reach).astype(kind)


def setup_inputs(seed: int = 0) -> dict:
    splits = jax.random.split(jax.random.key(seed), 19)
    tokens = noise(splits[0], (TOKENS, D), 1.0, 6.0, ((0, 32),))
    segment = draw_segment(jax.random.fold_in(splits[18], 71), 0)
    cotangent = gaussian_with(splits[2], (TOKENS, D), 1.0, 6.0, ((0, 32),), (0, 1, 32, 2.75))
    attn_norm_gain = jnp.clip(1.0 + 0.1 * jax.random.normal(splits[3], (D,), jnp.float32), 0.5, 1.5).astype(jnp.bfloat16)
    attn_norm_bias = noise(splits[4], (D,), 0.3, 1.75, ((0, 8),))
    qkv_weight = noise(splits[5], (D, 3 * D), D ** -0.5, 0.1875, ((0, 8),))
    query_bias = noise(splits[6], (D,), 0.5, 3.0, ((0, 8),))
    value_bias = noise(splits[7], (D,), 0.5, 3.0, ((0, 8),))
    proj_weight = noise(splits[8], (D, D), (max(1, 4 * D // IMG_LEN)) ** -0.5, 4.0, ((0, 8),))
    proj_bias = noise(splits[9], (D,), 0.3, 1.75, ((0, 8),))
    attn_scale = jnp.clip(jnp.exp(math.log(1.5) - 1.6133518 * jax.random.uniform(splits[10], (D,), jnp.float32) ** block_scale(splits[10], (D,), ((0, 8),), -0.2, 0.2)), 0.29882812, 1.5).astype(jnp.bfloat16)
    mlp_norm_gain = jnp.clip(1.0 + 0.1 * jax.random.normal(splits[11], (D,), jnp.float32), 0.5, 1.5).astype(jnp.bfloat16)
    mlp_norm_bias = noise(splits[12], (D,), 0.3, 1.75, ((0, 8),))
    hidden_weight = noise(splits[13], (D, FF), D ** -0.5, 0.1875, ((0, 8),))
    hidden_bias = noise(splits[14], (FF,), 0.3, 1.75, ((0, 8),))
    output_weight = noise(splits[15], (FF, D), FF ** -0.5, 0.09375, ((0, 8),))
    output_bias = noise(splits[16], (D,), 0.3, 1.75, ((0, 8),))
    mlp_scale = jnp.clip(jnp.exp(math.log(1.5) - 1.6133518 * jax.random.uniform(splits[17], (D,), jnp.float32) ** block_scale(splits[17], (D,), ((0, 8),), -0.2, 0.2)), 0.29882812, 1.5).astype(jnp.bfloat16)
    return {"tokens": tokens, "segment": segment, "cotangent": cotangent, "attn_norm_gain": attn_norm_gain, "attn_norm_bias": attn_norm_bias, "qkv_weight": qkv_weight, "query_bias": query_bias, "value_bias": value_bias, "proj_weight": proj_weight, "proj_bias": proj_bias, "attn_scale": attn_scale, "mlp_norm_gain": mlp_norm_gain, "mlp_norm_bias": mlp_norm_bias, "hidden_weight": hidden_weight, "hidden_bias": hidden_bias, "output_weight": output_weight, "output_bias": output_bias, "mlp_scale": mlp_scale}


EPS = 1e-06
NEG = -1e+30
HIGH = lax.Precision.HIGHEST

@jax.custom_vjp
def low(v):
    return lax.optimization_barrier(v.astype(jnp.bfloat16)).astype(jnp.float32)

@jax.custom_vjp
def low_back(v):
    return v

def low_keep(v):
    return (low(v), None)

def low_pass(kept, grad):
    return (grad,)

def back_keep(v):
    return (v, None)

def back_low(kept, grad):
    return (low(grad),)
low.defvjp(low_keep, low_pass)
low_back.defvjp(back_keep, back_low)

def layer_norm(matrix):
    average = lax.optimization_barrier(jnp.mean(matrix, axis=-1, keepdims=True))
    centred = matrix - average
    second_moment = lax.optimization_barrier(jnp.mean(centred * centred, axis=-1, keepdims=True))
    return centred * lax.rsqrt(second_moment + EPS)

def gelu_exact(values):
    return jax.nn.gelu(values, approximate=False)

def matmul_high(first_op, second_op):
    return jnp.dot(first_op, second_op, precision=HIGH, preferred_element_type=jnp.float32)

def attention(mixed_qkv, segment):
    queries = low_back(mixed_qkv[:, :D])
    key_rows = mixed_qkv[:, D:2 * D]
    value_rows = mixed_qkv[:, 2 * D:]
    margin = REACH * TOK_DEV
    window = (2 * REACH + 1) * TOK_DEV
    keys_padded = jnp.pad(key_rows, ((margin, margin), (0, 0)))
    values_padded = jnp.pad(value_rows, ((margin, margin), (0, 0)))
    ids_padded = jnp.pad(segment, (margin, margin), constant_values=-2)

    def one_block(block_index):
        row_start = block_index * TOK_DEV
        query_block = lax.dynamic_slice_in_dim(queries, row_start, TOK_DEV, 0).reshape(TOK_DEV, H, HD)
        key_block = low_back(lax.dynamic_slice_in_dim(keys_padded, row_start, window, 0)).reshape(window, H, HD)
        value_block = low_back(lax.dynamic_slice_in_dim(values_padded, row_start, window, 0)).reshape(window, H, HD)
        own_ids = lax.dynamic_slice_in_dim(segment, row_start, TOK_DEV, 0)
        near_ids = lax.dynamic_slice_in_dim(ids_padded, row_start, window, 0)
        row_at = lax.broadcasted_iota(jnp.int32, (TOK_DEV, window), 0)
        col_at = lax.broadcasted_iota(jnp.int32, (TOK_DEV, window), 1)
        same_image = (own_ids[:, None] == near_ids[None, :]) & (near_ids[None, :] >= 0)
        allowed = same_image | (row_at + margin == col_at)
        scores = low_back(jnp.einsum('qhd,khd->hqk', query_block, key_block, precision=HIGH) * HD ** (-0.5))
        scores = jnp.where(allowed[None], scores, NEG)
        row_peak = lax.optimization_barrier(jnp.max(scores, axis=2, keepdims=True))
        weights = jnp.exp(scores - row_peak)
        probability = weights / lax.optimization_barrier(jnp.sum(weights, axis=2, keepdims=True))
        result = jnp.einsum('hqk,khd->qhd', low(probability), value_block, precision=HIGH)
        return result.reshape(TOK_DEV, D)
    block_ids = jnp.arange(TOKENS // TOK_DEV, dtype=jnp.int32)
    blocks = lax.map(jax.checkpoint(one_block), block_ids)
    return blocks.reshape(TOKENS, D)

def forward(inputs, segment, attn_norm_gain, attn_norm_bias, qkv_weight, query_bias, value_bias, proj_weight, proj_bias, attn_scale, mlp_norm_gain, mlp_norm_bias, hidden_weight, hidden_bias, output_weight, output_bias, mlp_scale):
    first_in = low(layer_norm(inputs) * attn_norm_gain + attn_norm_bias)
    bias_row = jnp.concatenate([query_bias, jnp.zeros_like(query_bias), value_bias])
    mixed_qkv = low(matmul_high(first_in, qkv_weight) + bias_row)
    attended = low_back(low(attention(mixed_qkv, segment)))
    branch_one = low_back(matmul_high(attended, proj_weight) + proj_bias)
    middle = inputs + attn_scale * branch_one
    second_in = low(layer_norm(middle) * mlp_norm_gain + mlp_norm_bias)
    hidden = low_back(matmul_high(second_in, hidden_weight) + hidden_bias)
    active = low(gelu_exact(hidden))
    branch_two = low_back(matmul_high(active, output_weight) + output_bias)
    return middle + mlp_scale * branch_two

def reference(tokens, segment, cotangent, attn_norm_gain, attn_norm_bias, qkv_weight, query_bias, value_bias, proj_weight, proj_bias, attn_scale, mlp_norm_gain, mlp_norm_bias, hidden_weight, hidden_bias, output_weight, output_bias, mlp_scale):
    params = tuple((argument.astype(jnp.float32) for argument in (attn_norm_gain, attn_norm_bias, qkv_weight, query_bias, value_bias, proj_weight, proj_bias, attn_scale, mlp_norm_gain, mlp_norm_bias, hidden_weight, hidden_bias, output_weight, output_bias, mlp_scale)))

    def run_layer(inputs, *weights):
        return forward(inputs, segment, *weights)
    result, pull = jax.vjp(run_layer, tokens.astype(jnp.float32), *params)
    grads = pull(cotangent.astype(jnp.float32))
    return (result.astype(jnp.bfloat16), grads[0], grads[1], grads[2], grads[3], grads[4], grads[5], grads[6], grads[7], grads[8], grads[9], grads[10], grads[11], grads[12], grads[13], grads[14], grads[15])
```

```python
import jax
import jax.numpy as jnp
from jax import lax
from jax.experimental import pallas as pl
from jax.experimental.pallas import tpu as pltpu
from jax.sharding import PartitionSpec as P

H = 16
HD = 64
REACH = 3
EPS = 1e-06
NEG = -1e30
LOG2E = 1.4426950408889634
Q_TILE = 256
K_TILE_FWD = 512
K_TILE_BWD = 256


def passed_along(value, axis, steps):
    count = lax.axis_size(axis)
    leading, last = (max(0, -steps), min(count, count - steps))
    return lax.ppermute(value, axis, [(source, source + steps) for source in range(leading, last)])


def layer_norm_parts(matrix):
    average = jnp.mean(matrix, axis=-1, keepdims=True)
    centred = matrix - average
    second_moment = jnp.mean(centred * centred, axis=-1, keepdims=True)
    inverse = lax.rsqrt(second_moment + EPS)
    return centred * inverse, inverse


def layer_norm_back(grad, normed, inverse):
    first = jnp.mean(grad, axis=-1, keepdims=True)
    second = jnp.mean(grad * normed, axis=-1, keepdims=True)
    return (grad - first - normed * second) * inverse


def plain_dot(first_op, second_op):
    return jnp.dot(first_op, second_op, preferred_element_type=jnp.float32)


def dot_first_t(first_op, second_op):
    return lax.dot_general(
        first_op, second_op, (((0,), (0,)), ((), ())), preferred_element_type=jnp.float32
    )


def dot_second_t(first_op, second_op):
    return lax.dot_general(
        first_op, second_op, (((1,), (1,)), ((), ())), preferred_element_type=jnp.float32
    )


def column_sum(matrix):
    return jnp.sum(matrix.astype(jnp.float32), axis=0)


def as_float(vector):
    return vector.astype(jnp.float32)


def two_heads(block):
    low_half = lax.broadcasted_iota(jnp.int32, block.shape, 1) < HD
    zero = jnp.zeros_like(block)
    return jnp.concatenate([jnp.where(low_half, block, zero), jnp.where(low_half, zero, block)], axis=0)


def twice(row):
    return jnp.concatenate([row, row], axis=1)


def attend_kernel(limits, q_ref, kv_ref, cq_ref, ck_ref, o_ref, lse_ref):
    rows = q_ref.shape[0]
    step = K_TILE_FWD
    per_block = rows // step
    for tile in range(rows // Q_TILE):
        here = pl.ds(tile * Q_TILE, Q_TILE)
        q_pair = two_heads(q_ref[here, :])
        codes = twice(cq_ref[:, here])

        def body(index, carry):
            peak, total, acc = carry
            block = index // per_block
            place = pl.ds((index % per_block) * step, step)
            keys = kv_ref[block, 0, place, :]
            values_t = kv_ref[block, 1, place, :].T
            same = ck_ref[pl.ds(pl.multiple_of(index * step, step), step), :] == codes
            scores = dot_second_t(keys, q_pair) * (HD ** (-0.5) * LOG2E)
            scores = jnp.where(same, scores, NEG)
            new_peak = jnp.maximum(peak, jnp.max(scores, axis=0, keepdims=True))
            weights = jnp.exp2(scores - new_peak)
            decay = jnp.exp2(peak - new_peak)
            total = total * decay + jnp.sum(weights, axis=0, keepdims=True)
            low = weights.astype(jnp.bfloat16)
            part = jnp.concatenate(
                [
                    plain_dot(values_t[:HD, :], low[:, :Q_TILE]),
                    plain_dot(values_t[HD:, :], low[:, Q_TILE:]),
                ],
                axis=1,
            )
            return new_peak, total, acc * decay + part

        start = (
            jnp.full((1, 2 * Q_TILE), NEG, jnp.float32),
            jnp.zeros((1, 2 * Q_TILE), jnp.float32),
            jnp.zeros((HD, 2 * Q_TILE), jnp.float32),
        )
        first = limits[2 * tile] // (step // K_TILE_BWD)
        last = (limits[2 * tile + 1] + step // K_TILE_BWD - 1) // (step // K_TILE_BWD)
        peak, total, acc = lax.fori_loop(first, last, body, start)
        acc = acc / total
        o_ref[here, :] = jnp.concatenate([acc[:, :Q_TILE], acc[:, Q_TILE:]], axis=0).T
        lse_ref[0, :, pl.ds(tile * 2 * Q_TILE, 2 * Q_TILE)] = peak + jnp.log(total) * LOG2E


def attend_back_kernel(
    limits, q_ref, kv_ref, go_ref, o_ref, lse_ref, cq_ref, ck_ref, dq_ref, dkv_ref, acc_ref
):
    rows = q_ref.shape[0]
    step = K_TILE_BWD
    per_block = rows // step
    score_scale = HD ** (-0.5)
    acc_ref[...] = jnp.zeros_like(acc_ref)
    for tile in range(rows // Q_TILE):
        here = pl.ds(tile * Q_TILE, Q_TILE)
        q_pair = two_heads(q_ref[here, :])
        go = go_ref[here, :]
        go_pair = two_heads(go)
        inner = (go.astype(jnp.float32) * o_ref[here, :]).T
        inner = jnp.concatenate(
            [
                jnp.sum(inner[:HD, :], axis=0, keepdims=True),
                jnp.sum(inner[HD:, :], axis=0, keepdims=True),
            ],
            axis=1,
        )
        lse = lse_ref[0, :, pl.ds(tile * 2 * Q_TILE, 2 * Q_TILE)]
        codes = twice(cq_ref[:, here])

        def body(index, dq):
            block = index // per_block
            place = pl.ds((index % per_block) * step, step)
            keys = kv_ref[block, 0, place, :]
            values = kv_ref[block, 1, place, :]
            keys_t = keys.T
            same = ck_ref[pl.ds(pl.multiple_of(index * step, step), step), :] == codes
            scores = dot_second_t(keys, q_pair) * (score_scale * LOG2E)
            weights = jnp.where(same, jnp.exp2(scores - lse), 0.0)
            g_weights = dot_second_t(values, go_pair)
            g_scores = (weights * (g_weights - inner)).astype(jnp.bfloat16)
            acc_ref[block, 1, place, :] += plain_dot(weights.astype(jnp.bfloat16), go_pair)
            acc_ref[block, 0, place, :] += plain_dot(g_scores, q_pair)
            part = jnp.concatenate(
                [
                    plain_dot(keys_t[:HD, :], g_scores[:, :Q_TILE]),
                    plain_dot(keys_t[HD:, :], g_scores[:, Q_TILE:]),
                ],
                axis=0,
            )
            return dq + part

        dq = lax.fori_loop(
            limits[2 * tile],
            limits[2 * tile + 1],
            body,
            jnp.zeros((2 * HD, Q_TILE), jnp.float32),
        )
        dq_ref[here, :] = (dq * score_scale).T.astype(jnp.bfloat16)
    dkv_ref[:, 0, :, :] = (acc_ref[:, 0, :, :] * score_scale).astype(jnp.bfloat16)
    dkv_ref[:, 1, :, :] = acc_ref[:, 1, :, :].astype(jnp.bfloat16)


def attend(limits, queries, near, own_codes, near_codes):
    rows, width = queries.shape
    blocks = near.shape[0]
    pairs = width // (2 * HD)
    lanes = 2 * HD
    column = pl.BlockSpec((rows, lanes), lambda p, lim: (0, p))
    return pl.pallas_call(
        attend_kernel,
        grid_spec=pltpu.PrefetchScalarGridSpec(
            num_scalar_prefetch=1,
            grid=(pairs,),
            in_specs=[
                column,
                pl.BlockSpec((blocks, 2, rows, lanes), lambda p, lim: (0, 0, 0, p)),
                pl.BlockSpec((1, rows), lambda p, lim: (0, 0)),
                pl.BlockSpec((blocks * rows, 1), lambda p, lim: (0, 0)),
            ],
            out_specs=[column, pl.BlockSpec((1, 1, 2 * rows), lambda p, lim: (p, 0, 0))],
        ),
        out_shape=[
            jax.ShapeDtypeStruct((rows, width), jnp.float32),
            jax.ShapeDtypeStruct((pairs, 1, 2 * rows), jnp.float32),
        ],
        compiler_params=pltpu.CompilerParams(vmem_limit_bytes=48 * 2**20),
        cost_estimate=pl.CostEstimate(
            flops=16 * rows * rows * blocks * width // 2,
            bytes_accessed=2 * blocks * 2 * rows * width,
            transcendentals=0,
        ),
    )(limits, queries, near, own_codes[None, :], near_codes[:, None])


def attend_back(limits, queries, near, g_out, out, lse, own_codes, near_codes):
    rows, width = queries.shape
    blocks = near.shape[0]
    pairs = width // (2 * HD)
    lanes = 2 * HD
    column = pl.BlockSpec((rows, lanes), lambda p, lim: (0, p))
    window = pl.BlockSpec((blocks, 2, rows, lanes), lambda p, lim: (0, 0, 0, p))
    return pl.pallas_call(
        attend_back_kernel,
        grid_spec=pltpu.PrefetchScalarGridSpec(
            num_scalar_prefetch=1,
            grid=(pairs,),
            in_specs=[
                column,
                window,
                column,
                column,
                pl.BlockSpec((1, 1, 2 * rows), lambda p, lim: (p, 0, 0)),
                pl.BlockSpec((1, rows), lambda p, lim: (0, 0)),
                pl.BlockSpec((blocks * rows, 1), lambda p, lim: (0, 0)),
            ],
            out_specs=[column, window],
            scratch_shapes=[pltpu.VMEM((blocks, 2, rows, lanes), jnp.float32)],
        ),
        out_shape=[
            jax.ShapeDtypeStruct((rows, width), jnp.bfloat16),
            jax.ShapeDtypeStruct((blocks, 2, rows, width), jnp.bfloat16),
        ],
        compiler_params=pltpu.CompilerParams(vmem_limit_bytes=48 * 2**20),
        cost_estimate=pl.CostEstimate(
            flops=40 * rows * rows * blocks * width // 2,
            bytes_accessed=4 * blocks * 2 * rows * width,
            transcendentals=0,
        ),
    )(limits, queries, near, g_out, out, lse, own_codes[None, :], near_codes[:, None])


def tile_limits(own_codes, near_codes):
    same = own_codes[:, None] == near_codes[None, :]
    queries = own_codes.shape[0] // Q_TILE
    count = near_codes.shape[0] // K_TILE_BWD
    touched = jnp.any(same.reshape(queries, Q_TILE, count, K_TILE_BWD), axis=(1, 3))
    number = jnp.arange(count, dtype=jnp.int32)[None, :]
    first = jnp.min(jnp.where(touched, number, count), axis=1)
    last = jnp.max(jnp.where(touched, number + 1, 0), axis=1)
    return jnp.stack([first, last], axis=1).reshape(-1)


def side_offsets():
    return [offset for offset in range(-REACH, REACH + 1) if offset != 0]


def gathered_rows(weight):
    return lax.all_gather(weight, "fsdp", axis=0, tiled=True)


def reduced_rows(grad):
    part = lax.psum_scatter(grad.astype(jnp.bfloat16), "fsdp", scatter_dimension=0, tiled=True)
    return lax.psum(part, "rep").astype(jnp.float32)


def local(
    tokens,
    segment,
    cotangent,
    attn_norm_gain,
    attn_norm_bias,
    qkv_weight,
    query_bias,
    value_bias,
    proj_weight,
    proj_bias,
    attn_scale,
    mlp_norm_gain,
    mlp_norm_bias,
    hidden_weight,
    hidden_bias,
    output_weight,
    output_bias,
    mlp_scale,
):
    both = ("rep", "fsdp")
    fsdp = lax.axis_size("fsdp")
    model_width = tokens.shape[1]
    tok_rows = tokens.shape[0]
    offsets = side_offsets()

    place = lax.axis_index(both) * tok_rows + lax.iota(jnp.int32, tok_rows)
    own_codes = jnp.where(segment >= 0, segment + 1, -1 - place)
    side_codes = {offset: passed_along(own_codes, both, -offset) for offset in offsets}
    side_codes[0] = own_codes
    near_codes = jnp.concatenate([side_codes[o] for o in range(-REACH, REACH + 1)])
    limits = tile_limits(own_codes, near_codes)

    vectors = (
        attn_norm_gain,
        attn_norm_bias,
        query_bias,
        value_bias,
        proj_bias,
        attn_scale,
        mlp_norm_gain,
        mlp_norm_bias,
        output_bias,
        mlp_scale,
        hidden_bias,
    )
    packed_vectors = as_float(lax.all_gather(jnp.concatenate(vectors), "fsdp", axis=0))
    whole = []
    at = 0
    for vector in vectors:
        size = vector.shape[0]
        whole.append(packed_vectors[:, at : at + size].reshape(-1))
        at += size
    (
        gain_one,
        shift_one,
        bias_query,
        bias_value,
        bias_proj,
        scale_one,
        gain_two,
        shift_two,
        bias_output,
        scale_two,
        bias_hidden,
    ) = whole
    w_qkv = gathered_rows(qkv_weight)
    w_proj = gathered_rows(proj_weight)
    w_hidden = gathered_rows(hidden_weight)
    w_output = gathered_rows(output_weight)

    inputs = as_float(tokens)
    normed_one, inverse_one = layer_norm_parts(inputs)
    first_in = (normed_one * gain_one + shift_one).astype(jnp.bfloat16)
    kv_plain = plain_dot(first_in, w_qkv[:, model_width:])
    packed = jnp.stack(
        [kv_plain[:, :model_width], kv_plain[:, model_width:] + bias_value]
    ).astype(jnp.bfloat16)
    sides = {offset: passed_along(packed, both, -offset) for offset in offsets}
    sides[0] = packed
    queries = (plain_dot(first_in, w_qkv[:, :model_width]) + bias_query).astype(jnp.bfloat16)
    near = jnp.stack([sides[o] for o in range(-REACH, REACH + 1)])

    attended_wide, lse = attend(limits, queries, near, own_codes, near_codes)
    attended = attended_wide.astype(jnp.bfloat16)
    branch_one = plain_dot(attended, w_proj) + bias_proj
    middle = inputs + scale_one * branch_one
    normed_two, inverse_two = layer_norm_parts(middle)
    second_in = (normed_two * gain_two + shift_two).astype(jnp.bfloat16)
    hidden = plain_dot(second_in, w_hidden) + bias_hidden
    cdf = 0.5 * (1.0 + lax.erf(hidden * (0.5**0.5)))
    density = jnp.exp(-0.5 * hidden * hidden) * 0.3989422804014327
    active, slope = lax.optimization_barrier(
        ((hidden * cdf).astype(jnp.bfloat16), (cdf + hidden * density).astype(jnp.bfloat16))
    )
    branch_two = plain_dot(active, w_output) + bias_output
    block_output = (middle + scale_two * branch_two).astype(jnp.bfloat16)

    upstream = as_float(cotangent)
    scale_two_grad = jnp.sum(upstream * branch_two, axis=0)
    g_branch_two = (scale_two * upstream).astype(jnp.bfloat16)
    output_weight_grad = dot_first_t(active, g_branch_two).astype(jnp.bfloat16)
    output_bias_grad = column_sum(g_branch_two)
    g_hidden = (dot_second_t(g_branch_two, w_output) * as_float(slope)).astype(jnp.bfloat16)
    g_hidden, output_weight_grad = lax.optimization_barrier((g_hidden, output_weight_grad))
    hidden_weight_grad = dot_first_t(second_in, g_hidden).astype(jnp.bfloat16)
    hidden_bias_grad = column_sum(g_hidden)
    g_second = dot_second_t(g_hidden, w_hidden)
    gain_two_grad = jnp.sum(g_second * normed_two, axis=0)
    shift_two_grad = jnp.sum(g_second, axis=0)
    g_middle = upstream + layer_norm_back(g_second * gain_two, normed_two, inverse_two)
    scale_one_grad = jnp.sum(g_middle * branch_one, axis=0)
    g_branch_one = (scale_one * g_middle).astype(jnp.bfloat16)
    proj_weight_grad = dot_first_t(attended, g_branch_one).astype(jnp.bfloat16)
    proj_bias_grad = column_sum(g_branch_one)
    g_attended = dot_second_t(g_branch_one, w_proj).astype(jnp.bfloat16)
    g_attended, hidden_weight_grad, proj_weight_grad = lax.optimization_barrier(
        (g_attended, hidden_weight_grad, proj_weight_grad)
    )
    output_weight_out = reduced_rows(output_weight_grad)
    hidden_weight_out = reduced_rows(hidden_weight_grad)
    proj_weight_out = reduced_rows(proj_weight_grad)

    g_query, g_near = attend_back(
        limits, queries, near, g_attended, attended_wide, lse, own_codes, near_codes
    )
    arrived = [passed_along(g_near[offset + REACH], both, offset) for offset in offsets]
    query_weight_grad = dot_first_t(first_in, g_query).astype(jnp.bfloat16)
    query_bias_grad = column_sum(g_query)
    g_first = dot_second_t(g_query, w_qkv[:, :model_width])
    g_kv = as_float(g_near[REACH])
    for piece in arrived:
        g_kv = g_kv + as_float(piece)
    value_bias_grad = jnp.sum(g_kv[1], axis=0)
    g_keys, g_values = g_kv[0].astype(jnp.bfloat16), g_kv[1].astype(jnp.bfloat16)
    g_kv_low = jnp.concatenate([g_keys, g_values], axis=1)
    kv_weight_grad = dot_first_t(first_in, g_kv_low).astype(jnp.bfloat16)
    g_first = g_first + dot_second_t(g_kv_low, w_qkv[:, model_width:])
    qkv_weight_out = jnp.concatenate(
        [reduced_rows(query_weight_grad), reduced_rows(kv_weight_grad)], axis=1
    )
    gain_one_grad = jnp.sum(g_first * normed_one, axis=0)
    shift_one_grad = jnp.sum(g_first, axis=0)
    input_grad = g_middle + layer_norm_back(g_first * gain_one, normed_one, inverse_one)

    small = (
        gain_one_grad,
        shift_one_grad,
        query_bias_grad,
        value_bias_grad,
        proj_bias_grad,
        scale_one_grad,
        gain_two_grad,
        shift_two_grad,
        output_bias_grad,
        scale_two_grad,
        hidden_bias_grad,
    )
    small_rows = jnp.concatenate([vector.reshape(fsdp, -1) for vector in small], axis=1)
    small_sum = lax.psum(
        lax.psum_scatter(small_rows, "fsdp", scatter_dimension=0, tiled=True), "rep"
    ).reshape(-1)
    owned = []
    at = 0
    for vector in small:
        size = vector.shape[0] // fsdp
        owned.append(small_sum[at : at + size])
        at += size
    return (
        block_output,
        input_grad,
        owned[0],
        owned[1],
        qkv_weight_out,
        owned[2],
        owned[3],
        proj_weight_out,
        owned[4],
        owned[5],
        owned[6],
        owned[7],
        hidden_weight_out,
        owned[10],
        output_weight_out,
        owned[8],
        owned[9],
    )


def solution(mesh):
    return jax.shard_map(
        local,
        mesh=mesh,
        in_specs=(
            P(("rep", "fsdp"), None),
            P(("rep", "fsdp")),
            P(("rep", "fsdp"), None),
            P("fsdp"),
            P("fsdp"),
            P("fsdp", None),
            P("fsdp"),
            P("fsdp"),
            P("fsdp", None),
            P("fsdp"),
            P("fsdp"),
            P("fsdp"),
            P("fsdp"),
            P("fsdp", None),
            P("fsdp"),
            P("fsdp", None),
            P("fsdp"),
            P("fsdp"),
        ),
        out_specs=(
            P(("rep", "fsdp"), None),
            P(("rep", "fsdp"), None),
            P("fsdp"),
            P("fsdp"),
            P("fsdp", None),
            P("fsdp"),
            P("fsdp"),
            P("fsdp", None),
            P("fsdp"),
            P("fsdp"),
            P("fsdp"),
            P("fsdp"),
            P("fsdp", None),
            P("fsdp"),
            P("fsdp", None),
            P("fsdp"),
            P("fsdp"),
        ),
        check_vma=False,
    )
```

```python
import jax
import jax.numpy as jnp
from jax import lax
from jax.experimental import pallas as pl
from jax.experimental.pallas import tpu as pltpu
from jax.sharding import PartitionSpec as P

H = 16
HD = 64
REACH = 3
EPS = 1e-06
NEG = -1e30
LOG2E = 1.4426950408889634
Q_TILE = 256
K_TILE_FWD = 512
K_TILE_BWD = 256


def passed_along(value, axis, steps):
    count = lax.axis_size(axis)
    leading, last = (max(0, -steps), min(count, count - steps))
    return lax.ppermute(value, axis, [(source, source + steps) for source in range(leading, last)])


def layer_norm_parts(matrix):
    average = jnp.mean(matrix, axis=-1, keepdims=True)
    centred = matrix - average
    second_moment = jnp.mean(centred * centred, axis=-1, keepdims=True)
    inverse = lax.rsqrt(second_moment + EPS)
    return centred * inverse, inverse


def layer_norm_back(grad, normed, inverse):
    first = jnp.mean(grad, axis=-1, keepdims=True)
    second = jnp.mean(grad * normed, axis=-1, keepdims=True)
    return (grad - first - normed * second) * inverse


def plain_dot(first_op, second_op):
    return jnp.dot(first_op, second_op, preferred_element_type=jnp.float32)


def dot_first_t(first_op, second_op):
    return lax.dot_general(
        first_op, second_op, (((0,), (0,)), ((), ())), preferred_element_type=jnp.float32
    )


def dot_second_t(first_op, second_op):
    return lax.dot_general(
        first_op, second_op, (((1,), (1,)), ((), ())), preferred_element_type=jnp.float32
    )


def column_sum(matrix):
    return jnp.sum(matrix.astype(jnp.float32), axis=0)


def as_float(vector):
    return vector.astype(jnp.float32)


def two_heads(block):
    low_half = lax.broadcasted_iota(jnp.int32, block.shape, 1) < HD
    zero = jnp.zeros_like(block)
    return jnp.concatenate([jnp.where(low_half, block, zero), jnp.where(low_half, zero, block)], axis=0)


def twice(row):
    return jnp.concatenate([row, row], axis=1)


def attend_kernel(limits, q_ref, kv_ref, cq_ref, ck_ref, o_ref, lse_ref):
    rows = q_ref.shape[1]
    step = K_TILE_FWD
    query_block = pl.program_id(0)
    per_block = rows // step
    for tile in range(rows // Q_TILE):
        here = pl.ds(tile * Q_TILE, Q_TILE)
        q_pair = two_heads(q_ref[0, here, :])
        codes = twice(cq_ref[0, :, here])

        def body(index, carry):
            peak, total, acc = carry
            block = index // per_block
            place = pl.ds((index % per_block) * step, step)
            keys = kv_ref[block, 0, place, :]
            values_t = kv_ref[block, 1, place, :].T
            same = ck_ref[pl.ds(pl.multiple_of(index * step, step), step), :] == codes
            scores = dot_second_t(keys, q_pair) * (HD ** (-0.5) * LOG2E)
            scores = jnp.where(same, scores, NEG)
            new_peak = jnp.maximum(peak, jnp.max(scores, axis=0, keepdims=True))
            weights = jnp.exp2(scores - new_peak)
            decay = jnp.exp2(peak - new_peak)
            total = total * decay + jnp.sum(weights, axis=0, keepdims=True)
            low = weights.astype(jnp.bfloat16)
            part = jnp.concatenate(
                [
                    plain_dot(values_t[:HD, :], low[:, :Q_TILE]),
                    plain_dot(values_t[HD:, :], low[:, Q_TILE:]),
                ],
                axis=1,
            )
            return new_peak, total, acc * decay + part

        start = (
            jnp.full((1, 2 * Q_TILE), NEG, jnp.float32),
            jnp.zeros((1, 2 * Q_TILE), jnp.float32),
            jnp.zeros((HD, 2 * Q_TILE), jnp.float32),
        )
        entry = 2 * (query_block * (rows // Q_TILE) + tile)
        first = limits[entry] // (step // K_TILE_BWD)
        last = (limits[entry + 1] + step // K_TILE_BWD - 1) // (step // K_TILE_BWD)
        peak, total, acc = lax.fori_loop(first, last, body, start)
        acc = acc / total
        o_ref[0, here, :] = jnp.concatenate([acc[:, :Q_TILE], acc[:, Q_TILE:]], axis=0).T
        lse_ref[0, :, pl.ds(tile * 2 * Q_TILE, 2 * Q_TILE)] = peak + jnp.log(total) * LOG2E


def attend_back_kernel(
    limits, q_ref, kv_ref, go_ref, o_ref, lse_ref, cq_ref, ck_ref, dq_ref, dkv_ref, acc_ref
):
    rows = q_ref.shape[1]
    step = K_TILE_BWD
    query_block = pl.program_id(0)
    per_block = rows // step
    score_scale = HD ** (-0.5)

    @pl.when(query_block == 0)
    def _():
        acc_ref[...] = jnp.zeros_like(acc_ref)

    for tile in range(rows // Q_TILE):
        here = pl.ds(tile * Q_TILE, Q_TILE)
        q_pair = two_heads(q_ref[0, here, :])
        go = go_ref[0, here, :]
        go_pair = two_heads(go)
        inner = (go.astype(jnp.float32) * o_ref[0, here, :]).T
        inner = jnp.concatenate(
            [
                jnp.sum(inner[:HD, :], axis=0, keepdims=True),
                jnp.sum(inner[HD:, :], axis=0, keepdims=True),
            ],
            axis=1,
        )
        lse = lse_ref[0, :, pl.ds(tile * 2 * Q_TILE, 2 * Q_TILE)]
        codes = twice(cq_ref[0, :, here])

        def body(index, dq):
            block = index // per_block
            place = pl.ds((index % per_block) * step, step)
            keys = kv_ref[block, 0, place, :]
            values = kv_ref[block, 1, place, :]
            keys_t = keys.T
            same = ck_ref[pl.ds(pl.multiple_of(index * step, step), step), :] == codes
            scores = dot_second_t(keys, q_pair) * (score_scale * LOG2E)
            weights = jnp.where(same, jnp.exp2(scores - lse), 0.0)
            g_weights = dot_second_t(values, go_pair)
            g_scores = (weights * (g_weights - inner)).astype(jnp.bfloat16)
            acc_ref[block, 1, place, :] += plain_dot(weights.astype(jnp.bfloat16), go_pair)
            acc_ref[block, 0, place, :] += plain_dot(g_scores, q_pair)
            part = jnp.concatenate(
                [
                    plain_dot(keys_t[:HD, :], g_scores[:, :Q_TILE]),
                    plain_dot(keys_t[HD:, :], g_scores[:, Q_TILE:]),
                ],
                axis=0,
            )
            return dq + part

        entry = 2 * (query_block * (rows // Q_TILE) + tile)
        dq = lax.fori_loop(
            limits[entry],
            limits[entry + 1],
            body,
            jnp.zeros((2 * HD, Q_TILE), jnp.float32),
        )
        dq_ref[0, here, :] = (dq * score_scale).T.astype(jnp.bfloat16)

    @pl.when(query_block == pl.num_programs(0) - 1)
    def _():
        dkv_ref[:, 0, :, :] = (acc_ref[:, 0, :, :] * score_scale).astype(jnp.bfloat16)
        dkv_ref[:, 1, :, :] = acc_ref[:, 1, :, :].astype(jnp.bfloat16)


def attend(limits, queries, near, own_codes, near_codes):
    blocks, rows, lanes = queries.shape
    column = pl.BlockSpec((1, rows, lanes), lambda b, lim: (b, 0, 0))
    return pl.pallas_call(
        attend_kernel,
        grid_spec=pltpu.PrefetchScalarGridSpec(
            num_scalar_prefetch=1,
            grid=(blocks,),
            in_specs=[
                column,
                pl.BlockSpec(near.shape, lambda b, lim: (0, 0, 0, 0)),
                pl.BlockSpec((1, 1, rows), lambda b, lim: (b, 0, 0)),
                pl.BlockSpec((near_codes.shape[0], 1), lambda b, lim: (0, 0)),
            ],
            out_specs=[column, pl.BlockSpec((1, 1, 2 * rows), lambda b, lim: (b, 0, 0))],
        ),
        out_shape=[
            jax.ShapeDtypeStruct((blocks, rows, lanes), jnp.float32),
            jax.ShapeDtypeStruct((blocks, 1, 2 * rows), jnp.float32),
        ],
        compiler_params=pltpu.CompilerParams(vmem_limit_bytes=50 * 2**20),
        cost_estimate=pl.CostEstimate(
            flops=64 * rows * rows * blocks * 4 * lanes,
            bytes_accessed=16 * blocks * rows * lanes,
            transcendentals=0,
        ),
    )(limits, queries, near, own_codes[:, None, :], near_codes[:, None])


def attend_back(limits, queries, near, g_out, out, lse, own_codes, near_codes):
    blocks, rows, lanes = queries.shape
    column = pl.BlockSpec((1, rows, lanes), lambda b, lim: (b, 0, 0))
    window = pl.BlockSpec(near.shape, lambda b, lim: (0, 0, 0, 0))
    return pl.pallas_call(
        attend_back_kernel,
        grid_spec=pltpu.PrefetchScalarGridSpec(
            num_scalar_prefetch=1,
            grid=(blocks,),
            in_specs=[
                column,
                window,
                column,
                column,
                pl.BlockSpec((1, 1, 2 * rows), lambda b, lim: (b, 0, 0)),
                pl.BlockSpec((1, 1, rows), lambda b, lim: (b, 0, 0)),
                pl.BlockSpec((near_codes.shape[0], 1), lambda b, lim: (0, 0)),
            ],
            out_specs=[column, window],
            scratch_shapes=[pltpu.VMEM(near.shape, jnp.float32)],
        ),
        out_shape=[
            jax.ShapeDtypeStruct((blocks, rows, lanes), jnp.bfloat16),
            jax.ShapeDtypeStruct(near.shape, jnp.bfloat16),
        ],
        compiler_params=pltpu.CompilerParams(vmem_limit_bytes=50 * 2**20),
        cost_estimate=pl.CostEstimate(
            flops=128 * rows * rows * blocks * 4 * lanes,
            bytes_accessed=32 * blocks * rows * lanes,
            transcendentals=0,
        ),
    )(limits, queries, near, g_out, out, lse, own_codes[:, None, :], near_codes[:, None])


def tile_limits(own_codes, near_codes):
    blocks, rows = own_codes.shape
    window = (2 * REACH + 1) * rows
    seen = jnp.stack([near_codes[b * rows : b * rows + window] for b in range(blocks)])
    same = own_codes[:, :, None] == seen[:, None, :]
    tiles, count = rows // Q_TILE, window // K_TILE_BWD
    touched = jnp.any(same.reshape(blocks, tiles, Q_TILE, count, K_TILE_BWD), axis=(2, 4))
    number = jnp.arange(count, dtype=jnp.int32)[None, None, :]
    first = jnp.min(jnp.where(touched, number, count), axis=2)
    last = jnp.max(jnp.where(touched, number + 1, 0), axis=2)
    shift = (jnp.arange(blocks, dtype=jnp.int32) * (rows // K_TILE_BWD))[:, None]
    return jnp.stack([first + shift, last + shift], axis=2).reshape(-1)


def regrouped(pieces, size):
    count = lax.axis_size("fsdp")
    groups = None
    if count != size:
        groups = [list(range(at, at + size)) for at in range(0, count, size)]
    return lax.all_to_all(pieces, "fsdp", 0, 0, axis_index_groups=groups)


def with_partner(value):
    count = lax.axis_size("rep")
    return lax.ppermute(value, "rep", [(at, at + 1 - 2 * (at % 2)) for at in range(count)])


def is_second():
    return lax.rem(lax.axis_index("rep"), 2) == 1


def halves(matrix):
    middle = matrix.shape[1] // 2
    left, right = matrix[:, :middle], matrix[:, middle:]
    second = is_second()
    return jnp.where(second, right, left), jnp.where(second, left, right)


def joined(mine, other):
    second = is_second()
    return jnp.concatenate(
        [jnp.where(second, other, mine), jnp.where(second, mine, other)], axis=1
    )


def gathered_rows(weight):
    mine, _ = halves(weight)
    whole = lax.all_gather(mine, "fsdp", axis=0, tiled=True)
    return joined(whole, with_partner(whole))


def reduced_half(grad):
    mine, other = halves(grad)
    total = (as_float(mine) + as_float(with_partner(other))).astype(jnp.bfloat16)
    return lax.psum_scatter(total, "fsdp", scatter_dimension=0, tiled=True)


def finished(parts):
    count = lax.axis_size("rep")
    groups = [list(range(core, count, 2)) for core in range(2)]
    flat = jnp.concatenate([part.reshape(-1, 128) for part in parts], axis=0)
    mine = lax.psum(flat, "rep", axis_index_groups=groups)
    other = with_partner(mine)
    results = []
    at = 0
    for part in parts:
        size = part.size // 128
        results.append(
            joined(mine[at : at + size].reshape(part.shape), other[at : at + size].reshape(part.shape)).astype(
                jnp.float32
            )
        )
        at += size
    return results


def local(
    tokens,
    segment,
    cotangent,
    attn_norm_gain,
    attn_norm_bias,
    qkv_weight,
    query_bias,
    value_bias,
    proj_weight,
    proj_bias,
    attn_scale,
    mlp_norm_gain,
    mlp_norm_bias,
    hidden_weight,
    hidden_bias,
    output_weight,
    output_bias,
    mlp_scale,
):
    both = ("rep", "fsdp")
    fsdp = lax.axis_size("fsdp")
    tok_rows, model_width = tokens.shape
    lanes = 2 * HD
    group = model_width // lanes

    place = lax.axis_index(both) * tok_rows + lax.iota(jnp.int32, tok_rows)
    codes = as_float(jnp.where(segment >= 0, segment + 1, -1 - place))
    vectors = (
        attn_norm_gain,
        attn_norm_bias,
        query_bias,
        value_bias,
        proj_bias,
        attn_scale,
        mlp_norm_gain,
        mlp_norm_bias,
        output_bias,
        mlp_scale,
        hidden_bias,
    )
    to_gather = jnp.concatenate([as_float(vector) for vector in vectors] + [codes])
    packed_vectors = lax.all_gather(to_gather, "fsdp", axis=0)
    whole = []
    at = 0
    for vector in vectors:
        size = vector.shape[0]
        whole.append(packed_vectors[:, at : at + size].reshape(-1))
        at += size
    (
        gain_one,
        shift_one,
        bias_query,
        bias_value,
        bias_proj,
        scale_one,
        gain_two,
        shift_two,
        bias_output,
        scale_two,
        bias_hidden,
    ) = whole
    first_of_group = lax.axis_index("fsdp") // group * group
    own_codes = lax.dynamic_slice_in_dim(packed_vectors[:, at:], first_of_group, group, 0)
    near_codes = jnp.concatenate(
        [
            passed_along(own_codes[group - REACH :], both, group),
            own_codes,
            passed_along(own_codes[:REACH], both, -group),
        ]
    ).reshape(-1)
    limits = tile_limits(own_codes, near_codes)
    w_qkv = gathered_rows(qkv_weight)
    w_proj = gathered_rows(proj_weight)
    w_hidden = gathered_rows(hidden_weight)
    w_output = gathered_rows(output_weight)

    inputs = as_float(tokens)
    normed_one, inverse_one = layer_norm_parts(inputs)
    first_in = (normed_one * gain_one + shift_one).astype(jnp.bfloat16)
    bias_row = jnp.concatenate([bias_query, jnp.zeros_like(bias_query), bias_value])
    mixed = (plain_dot(first_in, w_qkv) + bias_row).astype(jnp.bfloat16)
    mixed = mixed.reshape(tok_rows, 3, group, lanes).transpose(2, 1, 0, 3)
    mixed = regrouped(mixed, group)
    queries, packed = mixed[:, 0], mixed[:, 1:]
    near = jnp.concatenate(
        [
            passed_along(packed[group - REACH :], both, group),
            packed,
            passed_along(packed[:REACH], both, -group),
        ]
    )
    attended_wide, lse = attend(limits, queries, near, own_codes, near_codes)
    attended = regrouped(attended_wide.astype(jnp.bfloat16), group)
    attended = attended.transpose(1, 0, 2).reshape(tok_rows, model_width)
    branch_one = plain_dot(attended, w_proj) + bias_proj
    middle = inputs + scale_one * branch_one
    normed_two, inverse_two = layer_norm_parts(middle)
    second_in = (normed_two * gain_two + shift_two).astype(jnp.bfloat16)
    hidden = plain_dot(second_in, w_hidden) + bias_hidden
    cdf = 0.5 * (1.0 + lax.erf(hidden * (0.5**0.5)))
    density = jnp.exp(-0.5 * hidden * hidden) * 0.3989422804014327
    active, slope = lax.optimization_barrier(
        ((hidden * cdf).astype(jnp.bfloat16), (cdf + hidden * density).astype(jnp.bfloat16))
    )
    branch_two = plain_dot(active, w_output) + bias_output
    block_output = (middle + scale_two * branch_two).astype(jnp.bfloat16)

    upstream = as_float(cotangent)
    scale_two_grad = jnp.sum(upstream * branch_two, axis=0)
    g_branch_two = (scale_two * upstream).astype(jnp.bfloat16)
    output_weight_grad = dot_first_t(active, g_branch_two).astype(jnp.bfloat16)
    output_bias_grad = column_sum(g_branch_two)
    g_hidden = (dot_second_t(g_branch_two, w_output) * as_float(slope)).astype(jnp.bfloat16)
    g_hidden, output_weight_grad = lax.optimization_barrier((g_hidden, output_weight_grad))
    hidden_weight_grad = dot_first_t(second_in, g_hidden).astype(jnp.bfloat16)
    hidden_bias_grad = column_sum(g_hidden)
    g_second = dot_second_t(g_hidden, w_hidden)
    gain_two_grad = jnp.sum(g_second * normed_two, axis=0)
    shift_two_grad = jnp.sum(g_second, axis=0)
    g_middle = upstream + layer_norm_back(g_second * gain_two, normed_two, inverse_two)
    scale_one_grad = jnp.sum(g_middle * branch_one, axis=0)
    g_branch_one = (scale_one * g_middle).astype(jnp.bfloat16)
    proj_weight_grad = dot_first_t(attended, g_branch_one).astype(jnp.bfloat16)
    proj_bias_grad = column_sum(g_branch_one)
    g_attended = dot_second_t(g_branch_one, w_proj).astype(jnp.bfloat16)
    g_attended, hidden_weight_grad, proj_weight_grad = lax.optimization_barrier(
        (g_attended, hidden_weight_grad, proj_weight_grad)
    )
    output_weight_part = reduced_half(output_weight_grad)
    hidden_weight_part = reduced_half(hidden_weight_grad)
    proj_weight_part = reduced_half(proj_weight_grad)

    g_heads = regrouped(g_attended.reshape(tok_rows, group, lanes).transpose(1, 0, 2), group)
    g_query, g_near = attend_back(
        limits, queries, near, g_heads, attended_wide, lse, own_codes, near_codes
    )
    g_query, g_near, output_weight_part = lax.optimization_barrier(
        (g_query, g_near, output_weight_part)
    )
    from_next = passed_along(g_near[group + REACH :], both, group)
    from_last = passed_along(g_near[:REACH], both, -group)
    g_own = as_float(g_near[REACH : group + REACH])
    filler = jnp.zeros((group - REACH,) + g_own.shape[1:], jnp.float32)
    g_own = g_own + jnp.concatenate([as_float(from_next), filler])
    g_own = g_own + jnp.concatenate([filler, as_float(from_last)])
    g_mixed = jnp.concatenate([g_query[:, None], g_own.astype(jnp.bfloat16)], axis=1)
    g_mixed = regrouped(g_mixed, group).transpose(2, 1, 0, 3).reshape(tok_rows, 3 * model_width)
    qkv_weight_grad = dot_first_t(first_in, g_mixed).astype(jnp.bfloat16)
    qkv_weight_part = reduced_half(qkv_weight_grad)
    mixed_sums = column_sum(g_mixed)
    query_bias_grad = mixed_sums[:model_width]
    value_bias_grad = mixed_sums[2 * model_width :]
    g_first = dot_second_t(g_mixed, w_qkv)
    gain_one_grad = jnp.sum(g_first * normed_one, axis=0)
    shift_one_grad = jnp.sum(g_first, axis=0)
    input_grad = g_middle + layer_norm_back(g_first * gain_one, normed_one, inverse_one)

    small = (
        gain_one_grad,
        shift_one_grad,
        query_bias_grad,
        value_bias_grad,
        proj_bias_grad,
        scale_one_grad,
        gain_two_grad,
        shift_two_grad,
        output_bias_grad,
        scale_two_grad,
        hidden_bias_grad,
    )
    small_rows = jnp.concatenate([vector.reshape(fsdp, -1) for vector in small], axis=1)
    small_sum = lax.psum(
        lax.psum_scatter(small_rows, "fsdp", scatter_dimension=0, tiled=True), "rep"
    ).reshape(-1)
    qkv_weight_out, proj_weight_out, hidden_weight_out, output_weight_out = finished(
        (qkv_weight_part, proj_weight_part, hidden_weight_part, output_weight_part)
    )
    owned = []
    at = 0
    for vector in small:
        size = vector.shape[0] // fsdp
        owned.append(small_sum[at : at + size])
        at += size
    return (
        block_output,
        input_grad,
        owned[0],
        owned[1],
        qkv_weight_out,
        owned[2],
        owned[3],
        proj_weight_out,
        owned[4],
        owned[5],
        owned[6],
        owned[7],
        hidden_weight_out,
        owned[10],
        output_weight_out,
        owned[8],
        owned[9],
    )


def solution(mesh):
    return jax.shard_map(
        local,
        mesh=mesh,
        in_specs=(
            P(("rep", "fsdp"), None),
            P(("rep", "fsdp")),
            P(("rep", "fsdp"), None),
            P("fsdp"),
            P("fsdp"),
            P("fsdp", None),
            P("fsdp"),
            P("fsdp"),
            P("fsdp", None),
            P("fsdp"),
            P("fsdp"),
            P("fsdp"),
            P("fsdp"),
            P("fsdp", None),
            P("fsdp"),
            P("fsdp", None),
            P("fsdp"),
            P("fsdp"),
        ),
        out_specs=(
            P(("rep", "fsdp"), None),
            P(("rep", "fsdp"), None),
            P("fsdp"),
            P("fsdp"),
            P("fsdp", None),
            P("fsdp"),
            P("fsdp"),
            P("fsdp", None),
            P("fsdp"),
            P("fsdp"),
            P("fsdp"),
            P("fsdp"),
            P("fsdp", None),
            P("fsdp"),
            P("fsdp", None),
            P("fsdp"),
            P("fsdp"),
        ),
        check_vma=False,
    )
```
